256 devices in a mesh: blk: 32 (over x, y, z_hi), kv: 8 (over z_lo, core).
Axes of the slice: x: 4, y: 4, z: 8 (z_hi: 2, z_lo: 4; z = z_hi * 4 + z_lo), core: 2. Of those that a mesh axis runs over, the one named last changes fastest.
Arguments:
- queries: bfloat16 [16384, 1024], P(('blk', 'kv')), may hold values from -16 to 16
- keys: bfloat16 [16384, 1024], P(('blk', 'kv')), may hold values from -16 to 16
- values: bfloat16 [16384, 1024], P(('blk', 'kv')), may hold values from -6 to 6
- w_out: bfloat16 [1024, 1024], replicated, may hold values from -0.1875 to 0.1875
Outputs:
- encoded: bfloat16 [16384, 1024], P(('blk', 'kv'))
The draws below stay inside these ranges and needn't reach their ends.
All inputs are finite; a program needn't handle non-finite values.
Results may differ from the reference program's by a relative error of at most 0.01.
Values may be sent and summed in bfloat16 or wider, within the bound.
No kernel may reach another device: no remote copies, remote signals or barrier semaphores. Data moves between devices by JAX's collectives and lax.ppermute only.
A program may use at most 128 MiB of HBM per device.

```python
import jax
import jax.numpy as jnp
from jax import lax

HEADS = 16
HEAD_DIM = 64
D = 1024
ROWS = 64
TOKENS = 16384


def draw_queries(key, part):
    key = jax.random.fold_in(key, 11)
    result = jnp.clip(jax.random.normal(key, (TOKENS, D), jnp.float32), -4.0, 4.0)
    return result.astype(jnp.bfloat16)


def draw_keys(key, part):
    key = jax.random.fold_in(key, 23)
    result = jnp.clip(3.0 * jax.random.normal(key, (TOKENS, D), jnp.float32), -12.0, 12.0)
    return result.astype(jnp.bfloat16)


def block_scale(stream_key, shape, cuts, least, top_value):
    def one(position, shards_of):
        steps = jax.random.uniform(jax.random.fold_in(jax.random.fold_in(stream_key, 6), position), (shards_of,), jnp.float32, least / len(cuts), top_value / len(cuts))
        return jnp.repeat(jnp.exp(steps), shape[position] // shards_of).reshape((-1,) + (1,) * (len(shape) - position - 1))

    level = one(*cuts[0])
    for cut in cuts[1:]:
        level = level * one(*cut)
    return level


def gaussian(key, extent, scale, bound, cuts=(), held_as=jnp.bfloat16):
    loudness = block_scale(key, extent, cuts, -0.22, 0.18) if cuts else 1.0
    drawn = jax.random.normal(key, extent, jnp.float32) * scale * loudness
    return jnp.minimum(jnp.maximum(drawn, -bound), bound).astype(held_as)


def setup_inputs(seed: int = 0) -> dict:
    splits = jax.random.split(jax.random.key(seed), 5)
    return {
        "queries": draw_queries(jax.random.fold_in(splits[4], 71), 0),
        "keys": draw_keys(jax.random.fold_in(splits[4], 71), 0),
        "values": gaussian(splits[2], (TOKENS, D), 1.0, 6.0, ((0, 256),)),
        "w_out": gaussian(splits[3], (D, D), D ** -0.5, 0.1875),
    }


def reference(queries, keys, values, w_out):
    scaling = HEAD_DIM ** -0.5
    key_heads = keys.astype(jnp.float32).reshape(TOKENS, HEADS, HEAD_DIM)
    value_heads = values.astype(jnp.float32).reshape(TOKENS, HEADS, HEAD_DIM)
    query_blocks = queries.reshape(TOKENS // ROWS, ROWS, HEADS, HEAD_DIM)

    def attend(query_block):
        query_heads = query_block.astype(jnp.float32)
        scores = jnp.einsum("qhd,khd->hqk", query_heads, key_heads) * scaling
        highest = jnp.max(scores, axis=-1, keepdims=True)
        exact_probs = jnp.exp(scores - highest)
        totals = jnp.sum(exact_probs, axis=-1)
        rounded = lax.optimization_barrier(exact_probs.astype(jnp.bfloat16))
        weighted = jnp.einsum("hqk,khd->qhd", rounded.astype(jnp.float32), value_heads)
        normed = weighted / jnp.transpose(totals)[:, :, None]
        return normed.reshape(ROWS, D).astype(jnp.bfloat16)

    attended = lax.map(attend, query_blocks).reshape(TOKENS, D)
    return jnp.dot(attended, w_out, preferred_element_type=jnp.float32).astype(jnp.bfloat16)
```

```python
import functools

import jax
import jax.numpy as jnp
from jax import lax
from jax.experimental import pallas as pl
from jax.experimental.pallas import tpu as pltpu
from jax.sharding import Mesh, PartitionSpec as P

HEADS = 16
HEAD_DIM = 64
LANES = 128
STAT = HEAD_DIM
SHIFT = LANES - 1
LOG2E = 1.4426950408889634
BIG = 2.0**100
ROW_BLOCK = 256

NT = (((1,), (1,)), ((), ()))


def pack_kernel(q_hbm, k_hbm, v_hbm, out_ref, q_ref, k_ref, v_ref, sem):
    half = q_ref.shape[0] // 2
    copies = [
        pltpu.make_async_copy(source, target, sem.at[n])
        for n, (source, target) in enumerate(((k_hbm, k_ref), (v_hbm, v_ref), (q_hbm, q_ref)))
    ]
    for copy in copies:
        copy.start()
    for copy in copies:
        copy.wait()
    for head in range(HEADS):
        cols = slice(head * HEAD_DIM, (head + 1) * HEAD_DIM)
        kv = jnp.concatenate([k_ref[:, cols], v_ref[:, cols]], axis=1)
        q = q_ref[:, cols]
        q = jnp.concatenate([q[:half], q[half:]], axis=1)
        for core in range(2):
            out_ref[2 * head + core, :half, :] = kv[core * half : (core + 1) * half]
            out_ref[2 * head + core, half:, :] = q


def split_queries(q):
    stacked = jnp.concatenate([q[:, :HEAD_DIM], q[:, HEAD_DIM:]], axis=0).astype(jnp.float32)
    scaled = stacked * (LOG2E * HEAD_DIM**-0.5)
    high = scaled.astype(jnp.bfloat16)
    low = (scaled - high.astype(jnp.float32)).astype(jnp.bfloat16)
    return jnp.concatenate([high, low], axis=1)


def keys_twice(kv):
    return jnp.concatenate([kv[:, :HEAD_DIM], kv[:, :HEAD_DIM]], axis=1)


def values_and_one(kv):
    lane = lax.broadcasted_iota(jnp.int32, (kv.shape[0], HEAD_DIM), 1)
    one = jnp.where(lane == 0, 1.0, 0.0).astype(kv.dtype)
    return jnp.concatenate([kv[:, HEAD_DIM:], one], axis=1)


def with_shift(acc, shift):
    lane = lax.broadcasted_iota(jnp.int32, acc.shape, 1)
    return jnp.where(lane == SHIFT, shift, acc)


def scores(q_ref, rows, keys):
    return lax.dot_general(q_ref[rows, :], keys, NT, preferred_element_type=jnp.float32)


def first_kernel(core_ref, q_ref, kv_ref, q_own_ref, q_other_ref, own_ref, other_ref):
    core = core_ref[0]
    heads, _, rows, _ = q_ref.shape
    keys = keys_twice(kv_ref[...])
    values = values_and_one(kv_ref[...])
    for source, out_q_ref, acc_ref in (
        (core, q_own_ref, own_ref),
        (1 - core, q_other_ref, other_ref),
    ):
        out_q_ref[...] = split_queries(q_ref[:, source].reshape(heads * rows, LANES))
        for i in range(out_q_ref.shape[0] // ROW_BLOCK):
            rows_i = pl.ds(i * ROW_BLOCK, ROW_BLOCK)
            s = scores(out_q_ref, rows_i, keys)
            shift = jnp.max(s, axis=1, keepdims=True)
            p = jnp.exp2(s - shift).astype(jnp.bfloat16)
            acc_ref[rows_i, :] = with_shift(
                jnp.dot(p, values, preferred_element_type=jnp.float32), shift
            )


def absorb(q_ref, acc_in_ref, acc_ref, keys, values):
    for i in range(q_ref.shape[0] // ROW_BLOCK):
        rows = pl.ds(i * ROW_BLOCK, ROW_BLOCK)
        acc = acc_in_ref[rows, :]
        p = jnp.exp2(scores(q_ref, rows, keys) - acc[:, SHIFT:]).astype(jnp.bfloat16)
        acc_ref[rows, :] = acc + jnp.dot(p, values, preferred_element_type=jnp.float32)


def both(one_ref, two_ref):
    return jnp.concatenate([one_ref[...], two_ref[...]], axis=0)


def step_kernel(
    q_own_ref, q_other_ref, kv_one_ref, kv_two_ref, own_in_ref, other_in_ref, own_ref, other_ref
):
    kv = both(kv_one_ref, kv_two_ref)
    keys, values = keys_twice(kv), values_and_one(kv)
    absorb(q_own_ref, own_in_ref, own_ref, keys, values)
    absorb(q_other_ref, other_in_ref, other_ref, keys, values)


def in_range(acc_ref):
    return jnp.min(jnp.where(acc_ref[:, STAT : STAT + 1] < BIG, 1.0, 0.0)) > 0.5


def last_kernel(q_own_ref, q_other_ref, kv_one_ref, kv_two_ref, own_in_ref, other_in_ref, *refs):
    kv_refs, (own_ref, other_ref, kv_buf, sem) = refs[:-4], refs[-4:]
    refs = (q_own_ref, q_other_ref, kv_one_ref, kv_two_ref, own_in_ref, other_in_ref)
    step_kernel(*refs, own_ref, other_ref)

    @pl.when(jnp.logical_not(in_range(own_ref) & in_range(other_ref)))
    def _():
        for n, kv_ref in enumerate(kv_refs):
            size = kv_ref.shape[0]
            copy = pltpu.make_async_copy(kv_ref, kv_buf.at[:size], sem)
            copy.start()
            copy.wait()
            keys = keys_twice(kv_buf[:size])
            values = values_and_one(kv_buf[:size])
            for q_ref, acc_ref in ((q_own_ref, own_ref), (q_other_ref, other_ref)):

                def one(i, carry, q_ref=q_ref, acc_ref=acc_ref, keys=keys, values=values, n=n):
                    rows = pl.ds(pl.multiple_of(i * ROW_BLOCK, ROW_BLOCK), ROW_BLOCK)
                    s = scores(q_ref, rows, keys)
                    highest = jnp.max(s, axis=1, keepdims=True)
                    if n:
                        acc = acc_ref[rows, :]
                        before = acc[:, SHIFT:]
                        highest = jnp.maximum(highest, before)
                        acc = acc * jnp.exp2(before - highest)
                    p = jnp.exp2(s - highest).astype(jnp.bfloat16)
                    contrib = jnp.dot(p, values, preferred_element_type=jnp.float32)
                    acc_ref[rows, :] = with_shift(contrib + acc if n else contrib, highest)
                    return carry

                lax.fori_loop(0, q_ref.shape[0] // ROW_BLOCK, one, 0)


def merge_kernel(own_ref, other_ref, out_ref):
    own, other = own_ref[...], other_ref[...]
    a, b = own[:, SHIFT:], other[:, SHIFT:]
    top = jnp.maximum(a, b)
    both = own * jnp.exp2(a - top) + other * jnp.exp2(b - top)
    attended = (both[:, :HEAD_DIM] / both[:, STAT : STAT + 1]).astype(jnp.bfloat16)
    half = attended.shape[0] // 2
    out_ref[...] = jnp.concatenate([attended[:half], attended[half:]], axis=1).reshape(
        out_ref.shape
    )


def project_kernel(heads_ref, w_ref, out_ref):
    left = [heads_ref[h][:, :HEAD_DIM] for h in range(HEADS)]
    right = [heads_ref[h][:, HEAD_DIM:] for h in range(HEADS)]
    attended = jnp.concatenate(
        [jnp.concatenate(left, axis=1), jnp.concatenate(right, axis=1)], axis=0
    )
    out_ref[...] = jnp.dot(attended, w_ref[...], preferred_element_type=jnp.float32).astype(
        jnp.bfloat16
    )


def call(kernel, *shapes, vmem=24, **more):
    return pl.pallas_call(
        kernel,
        out_shape=shapes if len(shapes) > 1 else shapes[0],
        compiler_params=pltpu.CompilerParams(vmem_limit_bytes=vmem * 2**20),
        **more,
    )


def on_device(q, k, v, w_out):
    rows, width = q.shape
    half = rows // 2
    bf16, f32 = jnp.bfloat16, jnp.float32
    shape = jax.ShapeDtypeStruct
    vmem = pl.BlockSpec(memory_space=pltpu.VMEM)
    smem = pl.BlockSpec(memory_space=pltpu.SMEM)
    anywhere = pl.BlockSpec(memory_space=pl.ANY)

    packed = call(
        pack_kernel,
        shape((2 * HEADS, rows, LANES), bf16),
        vmem=56,
        in_specs=[anywhere] * 3,
        out_specs=vmem,
        scratch_shapes=[pltpu.VMEM((rows, width), bf16)] * 3 + [pltpu.SemaphoreType.DMA((3,))],
    )(q, k, v)
    mine = lax.all_to_all(packed, ("x", "y", "c"), 0, 0, tiled=True)
    count = HEADS * rows
    kv = mine[:, :half].reshape(count, LANES)
    q_mine = mine[:, half:].reshape(HEADS, 2, half, LANES)
    core = lax.axis_index("c").astype(jnp.int32).reshape(1)

    deep = lax.axis_size("zh") * lax.axis_size("zl")

    pairings = (
        [(z, z ^ 1) for z in range(deep)],
        [(z, ((z - 1) ^ 1) + 1 if z else deep - 1) for z in range(deep - 1)] + [(deep - 1, 0)],
    )

    def exchanged(first, second):
        return tuple(
            lax.ppermute(block, ("zh", "zl"), pairs)
            for block, pairs in zip((first, second), pairings)
        )

    def cost(queries, blocks):
        return pl.CostEstimate(
            flops=2 * 2 * queries * count * 2 * LANES * blocks,
            bytes_accessed=4 * 2**20,
            transcendentals=queries * count * blocks,
        )

    q_shape, acc_shape = shape((count, LANES), bf16), shape((count, LANES), f32)
    moving = exchanged(kv, kv)
    q_own, q_other, own, other = call(
        first_kernel,
        q_shape,
        q_shape,
        acc_shape,
        acc_shape,
        in_specs=[smem, vmem, vmem],
        out_specs=(vmem,) * 4,
        cost_estimate=cost(2 * count, 1),
    )(core, q_mine, kv)
    blocks = [kv]
    for hop in range(1, deep // 2):
        up, down, own, other = lax.optimization_barrier((*moving, own, other))
        blocks += [up, down]
        if hop + 1 < deep // 2:
            moving = exchanged(down, up)
        else:
            moving = exchanged(down[: count // 2], up[count // 2 :])
        own, other = call(
            step_kernel,
            acc_shape,
            acc_shape,
            cost_estimate=cost(2 * count, 2),
            input_output_aliases={4: 0, 5: 1},
        )(q_own, q_other, up, down, own, other)
    blocks += moving
    own, other = call(
        last_kernel,
        acc_shape,
        acc_shape,
        in_specs=[vmem] * 6 + [anywhere] * len(blocks),
        out_specs=(vmem, vmem),
        scratch_shapes=[pltpu.VMEM((count, LANES), bf16), pltpu.SemaphoreType.DMA],
        cost_estimate=cost(2 * count, 1),
        input_output_aliases={4: 0, 5: 1},
    )(q_own, q_other, *moving, own, other, *blocks)
    arrived = lax.ppermute(other, "c", [(0, 1), (1, 0)])
    attended = call(merge_kernel, shape((HEADS, half, LANES), bf16))(own, arrived)
    heads = lax.all_to_all(attended, ("x", "y"), 0, 0, tiled=True)
    return call(project_kernel, shape((rows, width), bf16))(heads, w_out)


def solution(mesh):
    axes = ("x", "y", "zh", "zl", "c")
    fine = Mesh(mesh.devices.reshape(4, 4, 2, 4, 2), axes)
    return jax.shard_map(
        on_device,
        mesh=fine,
        in_specs=(P(axes, None), P(axes, None), P(axes, None), P()),
        out_specs=P(axes, None),
        check_vma=False,
    )
```

```python
import functools

import jax
import jax.numpy as jnp
from jax import lax
from jax.experimental import pallas as pl
from jax.experimental.pallas import tpu as pltpu
from jax.sharding import Mesh, PartitionSpec as P

HEADS = 16
HEAD_DIM = 64
LANES = 128
STAT = HEAD_DIM
SHIFT = LANES - 1
LOG2E = 1.4426950408889634
BIG = 2.0**100
ROW_BLOCK = 256

NT = (((1,), (1,)), ((), ()))


def pack_kernel(q_hbm, k_hbm, v_hbm, out_ref, q_ref, k_ref, v_ref, sem):
    rows = q_ref.shape[0]
    half = rows // 2
    copies = [
        pltpu.make_async_copy(source, target, sem.at[n])
        for n, (source, target) in enumerate(((k_hbm, k_ref), (v_hbm, v_ref), (q_hbm, q_ref)))
    ]
    for copy in copies:
        copy.start()
    for copy in copies:
        copy.wait()
    for head in range(HEADS):
        cols = slice(head * HEAD_DIM, (head + 1) * HEAD_DIM)
        out_ref[head, :rows, :] = jnp.concatenate([k_ref[:, cols], v_ref[:, cols]], axis=1)
        q = q_ref[:, cols]
        out_ref[head, rows:, :] = jnp.concatenate([q[:half], q[half:]], axis=1)


def split_queries(q):
    stacked = jnp.concatenate([q[:, :HEAD_DIM], q[:, HEAD_DIM:]], axis=0).astype(jnp.float32)
    scaled = stacked * (LOG2E * HEAD_DIM**-0.5)
    high = scaled.astype(jnp.bfloat16)
    low = (scaled - high.astype(jnp.float32)).astype(jnp.bfloat16)
    return jnp.concatenate([high, low], axis=1)


def keys_twice(kv):
    return jnp.concatenate([kv[:, :HEAD_DIM], kv[:, :HEAD_DIM]], axis=1)


def values_and_one(kv):
    lane = lax.broadcasted_iota(jnp.int32, (kv.shape[0], HEAD_DIM), 1)
    one = jnp.where(lane == 0, 1.0, 0.0).astype(kv.dtype)
    return jnp.concatenate([kv[:, HEAD_DIM:], one], axis=1)


def with_shift(acc, shift):
    lane = lax.broadcasted_iota(jnp.int32, acc.shape, 1)
    return jnp.where(lane == SHIFT, shift, acc)


def scores(q_ref, rows, keys):
    return lax.dot_general(q_ref[rows, :], keys, NT, preferred_element_type=jnp.float32)


def first_kernel(q_own_in_ref, q_other_in_ref, kv_ref, q_own_ref, q_other_ref, own_ref, other_ref):
    keys = keys_twice(kv_ref[...])
    values = values_and_one(kv_ref[...])
    for q_in_ref, q_ref, acc_ref in (
        (q_own_in_ref, q_own_ref, own_ref),
        (q_other_in_ref, q_other_ref, other_ref),
    ):
        heads, rows, _ = q_in_ref.shape
        q_ref[...] = split_queries(q_in_ref[...].reshape(heads * rows, LANES))
        for i in range(q_ref.shape[0] // ROW_BLOCK):
            rows_i = pl.ds(i * ROW_BLOCK, ROW_BLOCK)
            s = scores(q_ref, rows_i, keys)
            shift = jnp.max(s, axis=1, keepdims=True)
            p = jnp.exp2(s - shift).astype(jnp.bfloat16)
            acc_ref[rows_i, :] = with_shift(
                jnp.dot(p, values, preferred_element_type=jnp.float32), shift
            )


def absorb(q_ref, acc_in_ref, acc_ref, keys, values):
    for i in range(q_ref.shape[0] // ROW_BLOCK):
        rows = pl.ds(i * ROW_BLOCK, ROW_BLOCK)
        acc = acc_in_ref[rows, :]
        p = jnp.exp2(scores(q_ref, rows, keys) - acc[:, SHIFT:]).astype(jnp.bfloat16)
        acc_ref[rows, :] = acc + jnp.dot(p, values, preferred_element_type=jnp.float32)


def step_kernel(q_own_ref, q_other_ref, kv_ref, own_in_ref, other_in_ref, own_ref, other_ref):
    keys, values = keys_twice(kv_ref[...]), values_and_one(kv_ref[...])
    absorb(q_own_ref, own_in_ref, own_ref, keys, values)
    absorb(q_other_ref, other_in_ref, other_ref, keys, values)


def in_range(acc_ref):
    outside = jnp.where(acc_ref[...] < BIG, 0.0, 1.0)
    return jnp.max(jnp.sum(outside, axis=0, keepdims=True)) < 0.5


def last_kernel(q_own_ref, q_other_ref, kv_ref, own_in_ref, other_in_ref, *refs):
    kv_refs, (own_ref, other_ref, kv_buf, sem) = refs[:-4], refs[-4:]
    step_kernel(q_own_ref, q_other_ref, kv_ref, own_in_ref, other_in_ref, own_ref, other_ref)

    @pl.when(jnp.logical_not(in_range(own_ref) & in_range(other_ref)))
    def _():
        for n, kv_ref in enumerate(kv_refs):
            size = kv_ref.shape[0]
            copy = pltpu.make_async_copy(kv_ref, kv_buf.at[:size], sem)
            copy.start()
            copy.wait()
            keys = keys_twice(kv_buf[:size])
            values = values_and_one(kv_buf[:size])
            for q_ref, acc_ref in ((q_own_ref, own_ref), (q_other_ref, other_ref)):

                def one(i, carry, q_ref=q_ref, acc_ref=acc_ref, keys=keys, values=values, n=n):
                    rows = pl.ds(pl.multiple_of(i * ROW_BLOCK, ROW_BLOCK), ROW_BLOCK)
                    s = scores(q_ref, rows, keys)
                    highest = jnp.max(s, axis=1, keepdims=True)
                    if n:
                        acc = acc_ref[rows, :]
                        before = acc[:, SHIFT:]
                        highest = jnp.maximum(highest, before)
                        acc = acc * jnp.exp2(before - highest)
                    p = jnp.exp2(s - highest).astype(jnp.bfloat16)
                    contrib = jnp.dot(p, values, preferred_element_type=jnp.float32)
                    acc_ref[rows, :] = with_shift(contrib + acc if n else contrib, highest)
                    return carry

                lax.fori_loop(0, q_ref.shape[0] // ROW_BLOCK, one, 0)


def merge_kernel(own_ref, other_ref, out_ref):
    own, other = own_ref[...], other_ref[...]
    a, b = own[:, SHIFT:], other[:, SHIFT:]
    top = jnp.maximum(a, b)
    both = own * jnp.exp2(a - top) + other * jnp.exp2(b - top)
    attended = (both[:, :HEAD_DIM] / both[:, STAT : STAT + 1]).astype(jnp.bfloat16)
    half = attended.shape[0] // 2
    out_ref[...] = jnp.concatenate([attended[:half], attended[half:]], axis=1).reshape(
        out_ref.shape
    )


def project_kernel(heads_ref, w_ref, out_ref):
    left = [heads_ref[h][:, :HEAD_DIM] for h in range(HEADS)]
    right = [heads_ref[h][:, HEAD_DIM:] for h in range(HEADS)]
    attended = jnp.concatenate(
        [jnp.concatenate(left, axis=1), jnp.concatenate(right, axis=1)], axis=0
    )
    out_ref[...] = jnp.dot(attended, w_ref[...], preferred_element_type=jnp.float32).astype(
        jnp.bfloat16
    )


def call(kernel, *shapes, vmem=24, **more):
    return pl.pallas_call(
        kernel,
        out_shape=shapes if len(shapes) > 1 else shapes[0],
        compiler_params=pltpu.CompilerParams(vmem_limit_bytes=vmem * 2**20),
        **more,
    )


def on_device(q, k, v, w_out):
    rows, width = q.shape
    half = rows // 2
    bf16, f32 = jnp.bfloat16, jnp.float32
    shape = jax.ShapeDtypeStruct
    vmem = pl.BlockSpec(memory_space=pltpu.VMEM)
    anywhere = pl.BlockSpec(memory_space=pl.ANY)

    packed = call(
        pack_kernel,
        shape((HEADS, rows + half, LANES), bf16),
        vmem=56,
        in_specs=[anywhere] * 3,
        out_specs=vmem,
        scratch_shapes=[pltpu.VMEM((rows, width), bf16)] * 3 + [pltpu.SemaphoreType.DMA((3,))],
    )(q, k, v)
    mine = lax.all_to_all(packed, ("x", "y"), 0, 0, tiled=True)
    swap = [(0, 1), (1, 0)]
    count = HEADS * rows
    kv = mine[:, :rows].reshape(count, LANES)

    deep = lax.axis_size("zh") * lax.axis_size("zl")
    pairings = (
        lambda z: z ^ 1,
        lambda z: (z + 1) % deep if z % 2 else (z - 1) % deep,
    )

    def exchanged(block, hop):
        pairs = [
            (2 * z + c, 2 * pairings[(hop + c + 1) % 2](z) + c) for z in range(deep) for c in range(2)
        ]
        return lax.ppermute(block, ("zh", "zl", "c"), pairs)

    def cost(blocks):
        return pl.CostEstimate(
            flops=2 * 2 * 2 * count * count * 2 * LANES * blocks,
            bytes_accessed=4 * 2**20,
            transcendentals=2 * count * count * blocks,
        )

    q_shape, acc_shape = shape((count, LANES), bf16), shape((count, LANES), f32)
    first = exchanged(kv, 0)
    partners = lax.ppermute(mine, "c", swap)
    second = exchanged(partners[:, :rows].reshape(count, LANES), 0)
    q_own, q_other, own, other = call(
        first_kernel, q_shape, q_shape, acc_shape, acc_shape, cost_estimate=cost(1)
    )(mine[:, rows:], partners[:, rows:], kv)
    blocks = [kv]
    for hop in range(1, deep // 2):
        for chain in range(2):
            now, own, other = lax.optimization_barrier((second if chain else first, own, other))
            blocks.append(now)
            if chain == 0:
                first = exchanged(now, hop)
            elif hop + 1 < deep // 2:
                second = exchanged(now, hop)
            own, other = call(
                step_kernel,
                acc_shape,
                acc_shape,
                cost_estimate=cost(1),
                input_output_aliases={3: 0, 4: 1},
            )(q_own, q_other, now, own, other)
    moving = first
    blocks.append(moving)
    own, other = call(
        last_kernel,
        acc_shape,
        acc_shape,
        in_specs=[vmem] * 5 + [anywhere] * len(blocks),
        out_specs=(vmem, vmem),
        scratch_shapes=[pltpu.VMEM((count, LANES), bf16), pltpu.SemaphoreType.DMA],
        cost_estimate=cost(1),
        input_output_aliases={3: 0, 4: 1},
    )(q_own, q_other, moving, own, other, *blocks)
    arrived = lax.ppermute(other, "c", swap)
    attended = call(merge_kernel, shape((HEADS, half, LANES), bf16))(own, arrived)
    heads = lax.all_to_all(attended, ("x", "y"), 0, 0, tiled=True)
    return call(project_kernel, shape((rows, width), bf16))(heads, w_out)


def solution(mesh):
    axes = ("x", "y", "zh", "zl", "c")
    fine = Mesh(mesh.devices.reshape(4, 4, 2, 4, 2), axes)
    return jax.shard_map(
        on_device,
        mesh=fine,
        in_specs=(P(axes, None), P(axes, None), P(axes, None), P()),
        out_specs=P(axes, None),
        check_vma=False,
    )
```

```python
import functools

import jax
import jax.numpy as jnp
from jax import lax
from jax.experimental import pallas as pl
from jax.experimental.pallas import tpu as pltpu
from jax.sharding import Mesh, PartitionSpec as P

HEADS = 16
HEAD_DIM = 64
LANES = 128
STAT = HEAD_DIM
SHIFT = LANES - 1
LOG2E = 1.4426950408889634
BIG = 2.0**100
LOWEST = -1e30
ROW_BLOCK = 512

NT = (((1,), (1,)), ((), ()))


def pack_kernel(q_hbm, k_hbm, v_hbm, out_ref, q_ref, k_ref, v_ref, sem):
    rows = q_ref.shape[0]
    half = rows // 2
    copies = [
        pltpu.make_async_copy(source, target, sem.at[n])
        for n, (source, target) in enumerate(((k_hbm, k_ref), (v_hbm, v_ref), (q_hbm, q_ref)))
    ]
    for copy in copies:
        copy.start()
    for copy in copies:
        copy.wait()
    for head in range(HEADS):
        cols = slice(head * HEAD_DIM, (head + 1) * HEAD_DIM)
        out_ref[head, :rows, :] = jnp.concatenate([k_ref[:, cols], v_ref[:, cols]], axis=1)
        q = q_ref[:, cols]
        out_ref[head, rows:, :] = jnp.concatenate([q[:half], q[half:]], axis=1)


def split_queries(q):
    stacked = jnp.concatenate([q[:, :HEAD_DIM], q[:, HEAD_DIM:]], axis=0).astype(jnp.float32)
    scaled = stacked * (LOG2E * HEAD_DIM**-0.5)
    high = scaled.astype(jnp.bfloat16)
    low = (scaled - high.astype(jnp.float32)).astype(jnp.bfloat16)
    return jnp.concatenate([high, low], axis=1)


def keys_twice(kv):
    return jnp.concatenate([kv[:, :HEAD_DIM], kv[:, :HEAD_DIM]], axis=1)


def values_and_one(kv):
    lane = lax.broadcasted_iota(jnp.int32, (kv.shape[0], HEAD_DIM), 1)
    one = jnp.where(lane == 0, 1.0, 0.0).astype(kv.dtype)
    return jnp.concatenate([kv[:, HEAD_DIM:], one], axis=1)


def with_shift(acc, shift):
    lane = lax.broadcasted_iota(jnp.int32, acc.shape, 1)
    return jnp.where(lane == SHIFT, shift, acc)


def scores(q_ref, rows, keys):
    return lax.dot_general(q_ref[rows, :], keys, NT, preferred_element_type=jnp.float32)


def first_kernel(q_own_ref, q_other_ref, kv_ref, q_ref, acc_ref):
    heads, rows, _ = q_own_ref.shape
    count = 2 * heads * rows
    q_ref[:count, :] = split_queries(q_own_ref[...].reshape(heads * rows, LANES))
    q_ref[count:, :] = split_queries(q_other_ref[...].reshape(heads * rows, LANES))
    keys, values = keys_twice(kv_ref[...]), values_and_one(kv_ref[...])

    def one(rows):
        s = scores(q_ref, rows, keys)
        shift = jnp.max(s, axis=1, keepdims=True)
        p = jnp.exp2(s - shift).astype(jnp.bfloat16)
        acc_ref[rows, :] = with_shift(jnp.dot(p, values, preferred_element_type=jnp.float32), shift)

    each_row_block(q_ref, one)


def each_row_block(q_ref, step):
    def body(i, carry):
        step(pl.ds(pl.multiple_of(i * ROW_BLOCK, ROW_BLOCK), ROW_BLOCK))
        return carry

    lax.fori_loop(0, q_ref.shape[0] // ROW_BLOCK, body, 0)


def step_kernel(q_ref, kv_ref, acc_in_ref, acc_ref):
    keys, values = keys_twice(kv_ref[...]), values_and_one(kv_ref[...])

    def one(rows):
        acc = acc_in_ref[rows, :]
        p = jnp.exp2(scores(q_ref, rows, keys) - acc[:, SHIFT:]).astype(jnp.bfloat16)
        acc_ref[rows, :] = acc + jnp.dot(p, values, preferred_element_type=jnp.float32)

    each_row_block(q_ref, one)


def last_kernel(q_ref, kv_ref, acc_in_ref, *refs):
    kv_refs, (acc_ref, kv_buf, sem) = refs[:-3], refs[-3:]
    step_kernel(q_ref, kv_ref, acc_in_ref, acc_ref)
    outside = jnp.where(acc_ref[...] < BIG, 0.0, 1.0)
    fine = jnp.max(jnp.sum(outside, axis=0, keepdims=True)) < 0.5

    @pl.when(jnp.logical_not(fine))
    def _():
        acc_ref[...] = with_shift(jnp.zeros_like(acc_ref), LOWEST)
        for other_kv_ref in kv_refs:
            copy = pltpu.make_async_copy(other_kv_ref, kv_buf, sem)
            copy.start()
            copy.wait()
            redo_block(q_ref, kv_buf, acc_ref)


def redo_block(q_ref, kv_ref, acc_ref):
    keys, values = keys_twice(kv_ref[...]), values_and_one(kv_ref[...])

    def one(rows):
        s = scores(q_ref, rows, keys)
        acc = acc_ref[rows, :]
        before = acc[:, SHIFT:]
        highest = jnp.maximum(jnp.max(s, axis=1, keepdims=True), before)
        p = jnp.exp2(s - highest).astype(jnp.bfloat16)
        contrib = jnp.dot(p, values, preferred_element_type=jnp.float32)
        acc_ref[rows, :] = with_shift(acc * jnp.exp2(before - highest) + contrib, highest)

    each_row_block(q_ref, one)


def merge_kernel(own_ref, other_ref, out_ref):
    own, other = own_ref[...], other_ref[...]
    a, b = own[:, SHIFT:], other[:, SHIFT:]
    top = jnp.maximum(a, b)
    both = own * jnp.exp2(a - top) + other * jnp.exp2(b - top)
    attended = (both[:, :HEAD_DIM] / both[:, STAT : STAT + 1]).astype(jnp.bfloat16)
    half = attended.shape[0] // 2
    out_ref[...] = jnp.concatenate([attended[:half], attended[half:]], axis=1).reshape(
        out_ref.shape
    )


def project_kernel(heads_ref, w_ref, out_ref):
    left = [heads_ref[h][:, :HEAD_DIM] for h in range(HEADS)]
    right = [heads_ref[h][:, HEAD_DIM:] for h in range(HEADS)]
    attended = jnp.concatenate(
        [jnp.concatenate(left, axis=1), jnp.concatenate(right, axis=1)], axis=0
    )
    out_ref[...] = jnp.dot(attended, w_ref[...], preferred_element_type=jnp.float32).astype(
        jnp.bfloat16
    )


def call(kernel, *shapes, vmem=24, **more):
    return pl.pallas_call(
        kernel,
        out_shape=shapes if len(shapes) > 1 else shapes[0],
        compiler_params=pltpu.CompilerParams(vmem_limit_bytes=vmem * 2**20),
        **more,
    )


def on_device(q, k, v, w_out):
    rows, width = q.shape
    half = rows // 2
    bf16, f32 = jnp.bfloat16, jnp.float32
    shape = jax.ShapeDtypeStruct
    vmem = pl.BlockSpec(memory_space=pltpu.VMEM)
    anywhere = pl.BlockSpec(memory_space=pl.ANY)

    packed = call(
        pack_kernel,
        shape((HEADS, rows + half, LANES), bf16),
        vmem=56,
        in_specs=[anywhere] * 3,
        out_specs=vmem,
        scratch_shapes=[pltpu.VMEM((rows, width), bf16)] * 3 + [pltpu.SemaphoreType.DMA((3,))],
    )(q, k, v)
    mine = lax.all_to_all(packed, ("x", "y"), 0, 0, tiled=True)
    swap = [(0, 1), (1, 0)]
    count = HEADS * rows
    kv = mine[:, :rows].reshape(count, LANES)

    deep = lax.axis_size("zh") * lax.axis_size("zl")
    pairings = (
        lambda z: z ^ 1,
        lambda z: (z + 1) % deep if z % 2 else (z - 1) % deep,
    )

    def exchanged(block, hop):
        pairs = [
            (2 * z + c, 2 * pairings[(hop + c) % 2](z) + c) for z in range(deep) for c in range(2)
        ]
        return lax.ppermute(block, ("zh", "zl", "c"), pairs)

    def cost(blocks):
        return pl.CostEstimate(
            flops=2 * 2 * 2 * count * count * 2 * LANES * blocks,
            bytes_accessed=4 * 2**20,
            transcendentals=2 * count * count * blocks,
        )

    q_shape, acc_shape = shape((2 * count, LANES), bf16), shape((2 * count, LANES), f32)
    chains = [exchanged(kv, 0)]
    partners = lax.ppermute(mine, "c", swap)
    chains.append(exchanged(partners[:, :rows].reshape(count, LANES), 0))
    q_all, acc = call(first_kernel, q_shape, acc_shape, cost_estimate=cost(1))(
        mine[:, rows:], partners[:, rows:], kv
    )
    blocks = [kv]
    for hop in range(1, deep // 2):
        for n in range(2):
            now, acc = lax.optimization_barrier((chains[n], acc))
            blocks.append(now)
            if n == 0 or hop + 1 < deep // 2:
                chains[n] = exchanged(now, hop)
            acc = call(
                step_kernel, acc_shape, cost_estimate=cost(1), input_output_aliases={2: 0}
            )(q_all, now, acc)
    blocks.append(chains[0])
    acc = call(
        last_kernel,
        acc_shape,
        in_specs=[vmem] * 3 + [anywhere] * len(blocks),
        out_specs=vmem,
        scratch_shapes=[pltpu.VMEM((count, LANES), bf16), pltpu.SemaphoreType.DMA],
        cost_estimate=cost(1),
        input_output_aliases={2: 0},
    )(q_all, chains[0], acc, *blocks)
    arrived = lax.ppermute(acc[count:], "c", swap)
    own = acc[:count]
    attended = call(merge_kernel, shape((HEADS, half, LANES), bf16))(own, arrived)
    heads = lax.all_to_all(attended, ("x", "y"), 0, 0, tiled=True)
    return call(project_kernel, shape((rows, width), bf16))(heads, w_out)


def solution(mesh):
    axes = ("x", "y", "zh", "zl", "c")
    fine = Mesh(mesh.devices.reshape(4, 4, 2, 4, 2), axes)
    return jax.shard_map(
        on_device,
        mesh=fine,
        in_specs=(P(axes, None), P(axes, None), P(axes, None), P()),
        out_specs=P(axes, None),
        check_vma=False,
    )
```

```python
import functools

import jax
import jax.numpy as jnp
from jax import lax
from jax.experimental import pallas as pl
from jax.experimental.pallas import tpu as pltpu
from jax.sharding import Mesh, PartitionSpec as P

HEADS = 16
HEAD_DIM = 64
LANES = 128
STAT = HEAD_DIM
SHIFT = LANES - 1
LOG2E = 1.4426950408889634
BIG = 2.0**100
LOWEST = -1e30
ROW_BLOCK = 512
SHIFT_KEYS = 256

NT = (((1,), (1,)), ((), ()))


def pack_kernel(q_hbm, k_hbm, v_hbm, out_ref, q_ref, k_ref, v_ref, sem):
    rows = q_ref.shape[0]
    half = rows // 2
    copies = [
        pltpu.make_async_copy(source, target, sem.at[n])
        for n, (source, target) in enumerate(((k_hbm, k_ref), (v_hbm, v_ref), (q_hbm, q_ref)))
    ]
    for copy in copies:
        copy.start()
    for copy in copies:
        copy.wait()
    for head in range(HEADS):
        cols = slice(head * HEAD_DIM, (head + 1) * HEAD_DIM)
        out_ref[head, :rows, :] = jnp.concatenate([k_ref[:, cols], v_ref[:, cols]], axis=1)
        q = q_ref[:, cols]
        out_ref[head, rows:, :] = jnp.concatenate([q[:half], q[half:]], axis=1)


def split_queries(q):
    stacked = jnp.concatenate([q[:, :HEAD_DIM], q[:, HEAD_DIM:]], axis=0).astype(jnp.float32)
    scaled = stacked * (LOG2E * HEAD_DIM**-0.5)
    high = scaled.astype(jnp.bfloat16)
    low = (scaled - high.astype(jnp.float32)).astype(jnp.bfloat16)
    return jnp.concatenate([high, low], axis=1)


def keys_twice(kv):
    return jnp.concatenate([kv[:, :HEAD_DIM], kv[:, :HEAD_DIM]], axis=1)


def values_and_one(kv):
    lane = lax.broadcasted_iota(jnp.int32, (kv.shape[0], HEAD_DIM), 1)
    one = jnp.where(lane == 0, 1.0, 0.0).astype(kv.dtype)
    return jnp.concatenate([kv[:, HEAD_DIM:], one], axis=1)


def with_shift(acc, shift):
    lane = lax.broadcasted_iota(jnp.int32, acc.shape, 1)
    return jnp.where(lane == SHIFT, shift, acc)


def scores(q_ref, rows, keys):
    return lax.dot_general(q_ref[rows, :], keys, NT, preferred_element_type=jnp.float32)


def first_kernel(q_own_ref, q_other_ref, kv_ref, q_ref, acc_ref):
    heads, rows, _ = q_own_ref.shape
    count = 2 * heads * rows
    q_ref[:count, :] = split_queries(q_own_ref[...].reshape(heads * rows, LANES))
    q_ref[count:, :] = split_queries(q_other_ref[...].reshape(heads * rows, LANES))
    few = keys_twice(kv_ref[:SHIFT_KEYS, :])

    def begin(rows):
        shift = jnp.max(scores(q_ref, rows, few), axis=1, keepdims=True)
        acc_ref[rows, :] = with_shift(jnp.zeros((ROW_BLOCK, LANES), jnp.float32), shift)

    each_row_block(q_ref, begin)
    step_kernel(q_ref, kv_ref, acc_ref, acc_ref)


def each_row_block(q_ref, step):
    def body(i, carry):
        step(pl.ds(pl.multiple_of(i * ROW_BLOCK, ROW_BLOCK), ROW_BLOCK))
        return carry

    lax.fori_loop(0, q_ref.shape[0] // ROW_BLOCK, body, 0)


def step_kernel(q_ref, kv_ref, acc_in_ref, acc_ref):
    keys, values = keys_twice(kv_ref[...]), values_and_one(kv_ref[...])

    def one(rows):
        acc = acc_in_ref[rows, :]
        p = jnp.exp2(scores(q_ref, rows, keys) - acc[:, SHIFT:]).astype(jnp.bfloat16)
        acc_ref[rows, :] = acc + jnp.dot(p, values, preferred_element_type=jnp.float32)

    each_row_block(q_ref, one)


def last_kernel(q_ref, kv_ref, acc_in_ref, *refs):
    kv_refs, (acc_ref, kv_buf, sem) = refs[:-3], refs[-3:]
    step_kernel(q_ref, kv_ref, acc_in_ref, acc_ref)
    outside = jnp.where(acc_ref[...] < BIG, 0.0, 1.0)
    fine = jnp.max(jnp.sum(outside, axis=0, keepdims=True)) < 0.5

    @pl.when(jnp.logical_not(fine))
    def _():
        acc_ref[...] = with_shift(jnp.zeros_like(acc_ref), LOWEST)
        for other_kv_ref in kv_refs:
            copy = pltpu.make_async_copy(other_kv_ref, kv_buf, sem)
            copy.start()
            copy.wait()
            redo_block(q_ref, kv_buf, acc_ref)


def redo_block(q_ref, kv_ref, acc_ref):
    keys, values = keys_twice(kv_ref[...]), values_and_one(kv_ref[...])

    def one(rows):
        s = scores(q_ref, rows, keys)
        acc = acc_ref[rows, :]
        before = acc[:, SHIFT:]
        highest = jnp.maximum(jnp.max(s, axis=1, keepdims=True), before)
        p = jnp.exp2(s - highest).astype(jnp.bfloat16)
        contrib = jnp.dot(p, values, preferred_element_type=jnp.float32)
        acc_ref[rows, :] = with_shift(acc * jnp.exp2(before - highest) + contrib, highest)

    each_row_block(q_ref, one)


def merge_kernel(own_ref, other_ref, out_ref):
    own, other = own_ref[...], other_ref[...]
    a, b = own[:, SHIFT:], other[:, SHIFT:]
    top = jnp.maximum(a, b)
    both = own * jnp.exp2(a - top) + other * jnp.exp2(b - top)
    attended = (both[:, :HEAD_DIM] / both[:, STAT : STAT + 1]).astype(jnp.bfloat16)
    half = attended.shape[0] // 2
    out_ref[...] = jnp.concatenate([attended[:half], attended[half:]], axis=1).reshape(
        out_ref.shape
    )


def project_kernel(heads_ref, w_ref, out_ref):
    left = [heads_ref[h][:, :HEAD_DIM] for h in range(HEADS)]
    right = [heads_ref[h][:, HEAD_DIM:] for h in range(HEADS)]
    attended = jnp.concatenate(
        [jnp.concatenate(left, axis=1), jnp.concatenate(right, axis=1)], axis=0
    )
    out_ref[...] = jnp.dot(attended, w_ref[...], preferred_element_type=jnp.float32).astype(
        jnp.bfloat16
    )


def call(kernel, *shapes, vmem=24, **more):
    return pl.pallas_call(
        kernel,
        out_shape=shapes if len(shapes) > 1 else shapes[0],
        compiler_params=pltpu.CompilerParams(vmem_limit_bytes=vmem * 2**20),
        **more,
    )


def on_device(q, k, v, w_out):
    rows, width = q.shape
    half = rows // 2
    bf16, f32 = jnp.bfloat16, jnp.float32
    shape = jax.ShapeDtypeStruct
    vmem = pl.BlockSpec(memory_space=pltpu.VMEM)
    anywhere = pl.BlockSpec(memory_space=pl.ANY)

    packed = call(
        pack_kernel,
        shape((HEADS, rows + half, LANES), bf16),
        vmem=56,
        in_specs=[anywhere] * 3,
        out_specs=vmem,
        scratch_shapes=[pltpu.VMEM((rows, width), bf16)] * 3 + [pltpu.SemaphoreType.DMA((3,))],
    )(q, k, v)
    mine = lax.all_to_all(packed, ("x", "y"), 0, 0, tiled=True)
    swap = [(0, 1), (1, 0)]
    count = HEADS * rows
    kv = mine[:, :rows].reshape(count, LANES)

    deep = lax.axis_size("zh") * lax.axis_size("zl")
    pairings = (
        lambda z: z ^ 1,
        lambda z: (z + 1) % deep if z % 2 else (z - 1) % deep,
    )

    def exchanged(block, hop):
        pairs = [
            (2 * z + c, 2 * pairings[(hop + c) % 2](z) + c) for z in range(deep) for c in range(2)
        ]
        return lax.ppermute(block, ("zh", "zl", "c"), pairs)

    def cost(blocks):
        return pl.CostEstimate(
            flops=2 * 2 * 2 * count * count * 2 * LANES * blocks,
            bytes_accessed=4 * 2**20,
            transcendentals=2 * count * count * blocks,
        )

    q_shape, acc_shape = shape((2 * count, LANES), bf16), shape((2 * count, LANES), f32)
    chains = [exchanged(kv, 0)]
    partners = lax.ppermute(mine, "c", swap)
    chains.append(exchanged(partners[:, :rows].reshape(count, LANES), 0))
    q_all, acc = call(first_kernel, q_shape, acc_shape, cost_estimate=cost(1))(
        mine[:, rows:], partners[:, rows:], kv
    )
    blocks = [kv]
    for hop in range(1, deep // 2):
        for n in range(2):
            now, acc = lax.optimization_barrier((chains[n], acc))
            blocks.append(now)
            if n == 0 or hop + 1 < deep // 2:
                chains[n] = exchanged(now, hop)
            acc = call(
                step_kernel, acc_shape, cost_estimate=cost(1), input_output_aliases={2: 0}
            )(q_all, now, acc)
    blocks.append(chains[0])
    acc = call(
        last_kernel,
        acc_shape,
        in_specs=[vmem] * 3 + [anywhere] * len(blocks),
        out_specs=vmem,
        scratch_shapes=[pltpu.VMEM((count, LANES), bf16), pltpu.SemaphoreType.DMA],
        cost_estimate=cost(1),
        input_output_aliases={2: 0},
    )(q_all, chains[0], acc, *blocks)
    arrived = lax.ppermute(acc[count:], "c", swap)
    own = acc[:count]
    attended = call(merge_kernel, shape((HEADS, half, LANES), bf16))(own, arrived)
    heads = lax.all_to_all(attended, ("x", "y"), 0, 0, tiled=True)
    return call(project_kernel, shape((rows, width), bf16))(heads, w_out)


def solution(mesh):
    axes = ("x", "y", "zh", "zl", "c")
    fine = Mesh(mesh.devices.reshape(4, 4, 2, 4, 2), axes)
    return jax.shard_map(
        on_device,
        mesh=fine,
        in_specs=(P(axes, None), P(axes, None), P(axes, None), P()),
        out_specs=P(axes, None),
        check_vma=False,
    )
```

```python
import functools

import jax
import jax.numpy as jnp
from jax import lax
from jax.experimental import pallas as pl
from jax.experimental.pallas import tpu as pltpu
from jax.sharding import Mesh, PartitionSpec as P

HEADS = 16
HEAD_DIM = 64
LANES = 128
STAT = HEAD_DIM
SHIFT = LANES - 1
LOG2E = 1.4426950408889634
BIG = 2.0**100
LOWEST = -1e30
ROW_BLOCK = 1024
REDO_BLOCK = 256
SHIFT_KEYS = 128

NT = (((1,), (1,)), ((), ()))


def pack_kernel(q_hbm, k_hbm, v_hbm, out_ref, q_ref, k_ref, v_ref, sem):
    rows = q_ref.shape[0]
    half = rows // 2
    copies = [
        pltpu.make_async_copy(source, target, sem.at[n])
        for n, (source, target) in enumerate(((k_hbm, k_ref), (v_hbm, v_ref), (q_hbm, q_ref)))
    ]
    for copy in copies:
        copy.start()
    for copy in copies:
        copy.wait()
    for head in range(HEADS):
        cols = slice(head * HEAD_DIM, (head + 1) * HEAD_DIM)
        out_ref[head, :rows, :] = jnp.concatenate([k_ref[:, cols], v_ref[:, cols]], axis=1)
        q = q_ref[:, cols]
        out_ref[head, rows:, :] = jnp.concatenate([q[:half], q[half:]], axis=1)


def split_queries(q):
    stacked = jnp.concatenate([q[:, :HEAD_DIM], q[:, HEAD_DIM:]], axis=0).astype(jnp.float32)
    scaled = stacked * (LOG2E * HEAD_DIM**-0.5)
    high = scaled.astype(jnp.bfloat16)
    low = (scaled - high.astype(jnp.float32)).astype(jnp.bfloat16)
    return jnp.concatenate([high, low], axis=1)


def keys_twice(kv):
    return jnp.concatenate([kv[:, :HEAD_DIM], kv[:, :HEAD_DIM]], axis=1)


def values_and_one(kv):
    lane = lax.broadcasted_iota(jnp.int32, (kv.shape[0], HEAD_DIM), 1)
    one = jnp.where(lane == 0, 1.0, 0.0).astype(kv.dtype)
    return jnp.concatenate([kv[:, HEAD_DIM:], one], axis=1)


def with_shift(acc, shift):
    lane = lax.broadcasted_iota(jnp.int32, acc.shape, 1)
    return jnp.where(lane == SHIFT, shift, acc)


def scores(q_ref, rows, keys):
    return lax.dot_general(q_ref[rows, :], keys, NT, preferred_element_type=jnp.float32)


def first_kernel(q_own_ref, q_other_ref, kv_ref, q_ref, acc_ref):
    heads, rows, _ = q_own_ref.shape
    count = 2 * heads * rows
    q_ref[:count, :] = split_queries(q_own_ref[...].reshape(heads * rows, LANES))
    q_ref[count:, :] = split_queries(q_other_ref[...].reshape(heads * rows, LANES))
    few = keys_twice(kv_ref[:SHIFT_KEYS, :])

    def begin(rows):
        shift = jnp.max(scores(q_ref, rows, few), axis=1, keepdims=True)
        acc_ref[rows, :] = with_shift(jnp.zeros((ROW_BLOCK, LANES), jnp.float32), shift)

    each_row_block(q_ref, begin)
    step_kernel(q_ref, kv_ref, acc_ref, acc_ref)


def each_row_block(q_ref, step, size=ROW_BLOCK):
    def body(i, carry):
        step(pl.ds(pl.multiple_of(i * size, size), size))
        return carry

    lax.fori_loop(0, q_ref.shape[0] // size, body, 0)


def step_kernel(q_ref, kv_ref, acc_in_ref, acc_ref):
    keys, values = keys_twice(kv_ref[...]), values_and_one(kv_ref[...])

    def one(rows):
        acc = acc_in_ref[rows, :]
        p = jnp.exp2(scores(q_ref, rows, keys) - acc[:, SHIFT:]).astype(jnp.bfloat16)
        acc_ref[rows, :] = acc + jnp.dot(p, values, preferred_element_type=jnp.float32)

    each_row_block(q_ref, one)


def last_kernel(q_ref, kv_ref, acc_in_ref, *refs):
    kv_refs, (acc_ref, kv_buf, sem) = refs[:-3], refs[-3:]
    step_kernel(q_ref, kv_ref, acc_in_ref, acc_ref)
    outside = jnp.where(acc_ref[...] < BIG, 0.0, 1.0)
    fine = jnp.max(jnp.sum(outside, axis=0, keepdims=True)) < 0.5

    @pl.when(jnp.logical_not(fine))
    def _():
        acc_ref[...] = with_shift(jnp.zeros_like(acc_ref), LOWEST)
        for other_kv_ref in kv_refs:
            copy = pltpu.make_async_copy(other_kv_ref, kv_buf, sem)
            copy.start()
            copy.wait()
            redo_block(q_ref, kv_buf, acc_ref)


def redo_block(q_ref, kv_ref, acc_ref):
    keys, values = keys_twice(kv_ref[...]), values_and_one(kv_ref[...])

    def one(rows):
        s = scores(q_ref, rows, keys)
        acc = acc_ref[rows, :]
        before = acc[:, SHIFT:]
        highest = jnp.maximum(jnp.max(s, axis=1, keepdims=True), before)
        p = jnp.exp2(s - highest).astype(jnp.bfloat16)
        contrib = jnp.dot(p, values, preferred_element_type=jnp.float32)
        acc_ref[rows, :] = with_shift(acc * jnp.exp2(before - highest) + contrib, highest)

    each_row_block(q_ref, one, REDO_BLOCK)


def merge_kernel(own_ref, other_ref, out_ref):
    own, other = own_ref[...], other_ref[...]
    a, b = own[:, SHIFT:], other[:, SHIFT:]
    top = jnp.maximum(a, b)
    both = own * jnp.exp2(a - top) + other * jnp.exp2(b - top)
    attended = (both[:, :HEAD_DIM] / both[:, STAT : STAT + 1]).astype(jnp.bfloat16)
    half = attended.shape[0] // 2
    out_ref[...] = jnp.concatenate([attended[:half], attended[half:]], axis=1).reshape(
        out_ref.shape
    )


def project_kernel(heads_ref, w_ref, out_ref):
    left = [heads_ref[h][:, :HEAD_DIM] for h in range(HEADS)]
    right = [heads_ref[h][:, HEAD_DIM:] for h in range(HEADS)]
    attended = jnp.concatenate(
        [jnp.concatenate(left, axis=1), jnp.concatenate(right, axis=1)], axis=0
    )
    out_ref[...] = jnp.dot(attended, w_ref[...], preferred_element_type=jnp.float32).astype(
        jnp.bfloat16
    )


def call(kernel, *shapes, vmem=24, **more):
    return pl.pallas_call(
        kernel,
        out_shape=shapes if len(shapes) > 1 else shapes[0],
        compiler_params=pltpu.CompilerParams(vmem_limit_bytes=vmem * 2**20),
        **more,
    )


def on_device(q, k, v, w_out):
    rows, width = q.shape
    half = rows // 2
    bf16, f32 = jnp.bfloat16, jnp.float32
    shape = jax.ShapeDtypeStruct
    vmem = pl.BlockSpec(memory_space=pltpu.VMEM)
    anywhere = pl.BlockSpec(memory_space=pl.ANY)

    packed = call(
        pack_kernel,
        shape((HEADS, rows + half, LANES), bf16),
        vmem=56,
        in_specs=[anywhere] * 3,
        out_specs=vmem,
        scratch_shapes=[pltpu.VMEM((rows, width), bf16)] * 3 + [pltpu.SemaphoreType.DMA((3,))],
    )(q, k, v)
    mine = lax.all_to_all(packed, ("x", "y"), 0, 0, tiled=True)
    swap = [(0, 1), (1, 0)]
    count = HEADS * rows
    kv = mine[:, :rows].reshape(count, LANES)

    deep = lax.axis_size("zh") * lax.axis_size("zl")
    pairings = (
        lambda z: z ^ 1,
        lambda z: (z + 1) % deep if z % 2 else (z - 1) % deep,
    )

    def exchanged(block, hop):
        pairs = [
            (2 * z + c, 2 * pairings[(hop + c) % 2](z) + c) for z in range(deep) for c in range(2)
        ]
        return lax.ppermute(block, ("zh", "zl", "c"), pairs)

    def cost(blocks):
        return pl.CostEstimate(
            flops=2 * 2 * 2 * count * count * 2 * LANES * blocks,
            bytes_accessed=4 * 2**20,
            transcendentals=2 * count * count * blocks,
        )

    q_shape, acc_shape = shape((2 * count, LANES), bf16), shape((2 * count, LANES), f32)
    chains = [exchanged(kv, 0)]
    partners = lax.ppermute(mine, "c", swap)
    chains.append(exchanged(partners[:, :rows].reshape(count, LANES), 0))
    q_all, acc = call(first_kernel, q_shape, acc_shape, cost_estimate=cost(1))(
        mine[:, rows:], partners[:, rows:], kv
    )
    blocks = [kv]
    for hop in range(1, deep // 2):
        for n in range(2):
            now, acc = lax.optimization_barrier((chains[n], acc))
            blocks.append(now)
            if n == 0 or hop + 1 < deep // 2:
                chains[n] = exchanged(now, hop)
            acc = call(
                step_kernel, acc_shape, cost_estimate=cost(1), input_output_aliases={2: 0}
            )(q_all, now, acc)
    blocks.append(chains[0])
    acc = call(
        last_kernel,
        acc_shape,
        in_specs=[vmem] * 3 + [anywhere] * len(blocks),
        out_specs=vmem,
        scratch_shapes=[pltpu.VMEM((count, LANES), bf16), pltpu.SemaphoreType.DMA],
        cost_estimate=cost(1),
        input_output_aliases={2: 0},
    )(q_all, chains[0], acc, *blocks)
    arrived = lax.ppermute(acc[count:], "c", swap)
    own = acc[:count]
    attended = call(merge_kernel, shape((HEADS, half, LANES), bf16))(own, arrived)
    heads = lax.all_to_all(attended, ("x", "y"), 0, 0, tiled=True)
    return call(project_kernel, shape((rows, width), bf16))(heads, w_out)


def solution(mesh):
    axes = ("x", "y", "zh", "zl", "c")
    fine = Mesh(mesh.devices.reshape(4, 4, 2, 4, 2), axes)
    return jax.shard_map(
        on_device,
        mesh=fine,
        in_specs=(P(axes, None), P(axes, None), P(axes, None), P()),
        out_specs=P(axes, None),
        check_vma=False,
    )
```

```python
import functools

import jax
import jax.numpy as jnp
from jax import lax
from jax.experimental import pallas as pl
from jax.experimental.pallas import tpu as pltpu
from jax.sharding import Mesh, PartitionSpec as P

HEADS = 16
HEAD_DIM = 64
LANES = 128
STAT = HEAD_DIM
SHIFT = LANES - 1
LOG2E = 1.4426950408889634
BIG = 2.0**100
LOWEST = -1e30
ROW_BLOCK = 2048
REDO_BLOCK = 256
SHIFT_KEYS = 128

NT = (((1,), (1,)), ((), ()))


def pack_kernel(q_hbm, k_hbm, v_hbm, out_ref, q_ref, k_ref, v_ref, sem):
    rows = q_ref.shape[0]
    half = rows // 2
    copies = [
        pltpu.make_async_copy(source, target, sem.at[n])
        for n, (source, target) in enumerate(((k_hbm, k_ref), (v_hbm, v_ref), (q_hbm, q_ref)))
    ]
    for copy in copies:
        copy.start()
    for copy in copies:
        copy.wait()
    for head in range(HEADS):
        cols = slice(head * HEAD_DIM, (head + 1) * HEAD_DIM)
        out_ref[head, :rows, :] = jnp.concatenate([k_ref[:, cols], v_ref[:, cols]], axis=1)
        q = q_ref[:, cols]
        out_ref[head, rows:, :] = jnp.concatenate([q[:half], q[half:]], axis=1)


def split_queries(q):
    stacked = jnp.concatenate([q[:, :HEAD_DIM], q[:, HEAD_DIM:]], axis=0).astype(jnp.float32)
    scaled = stacked * (LOG2E * HEAD_DIM**-0.5)
    high = scaled.astype(jnp.bfloat16)
    low = (scaled - high.astype(jnp.float32)).astype(jnp.bfloat16)
    return jnp.concatenate([high, low], axis=1)


def keys_twice(kv):
    return jnp.concatenate([kv[:, :HEAD_DIM], kv[:, :HEAD_DIM]], axis=1)


def values_and_one(kv):
    lane = lax.broadcasted_iota(jnp.int32, (kv.shape[0], HEAD_DIM), 1)
    one = jnp.where(lane == 0, 1.0, 0.0).astype(kv.dtype)
    return jnp.concatenate([kv[:, HEAD_DIM:], one], axis=1)


def with_shift(acc, shift):
    lane = lax.broadcasted_iota(jnp.int32, acc.shape, 1)
    return jnp.where(lane == SHIFT, shift, acc)


def scores(q_ref, rows, keys):
    return lax.dot_general(q_ref[rows, :], keys, NT, preferred_element_type=jnp.float32)


def first_kernel(q_own_ref, q_other_ref, kv_ref, q_ref, acc_ref):
    heads, rows, _ = q_own_ref.shape
    count = 2 * heads * rows
    q_ref[:count, :] = split_queries(q_own_ref[...].reshape(heads * rows, LANES))
    q_ref[count:, :] = split_queries(q_other_ref[...].reshape(heads * rows, LANES))
    few = keys_twice(kv_ref[:SHIFT_KEYS, :])

    def begin(rows):
        shift = jnp.max(scores(q_ref, rows, few), axis=1, keepdims=True)
        acc_ref[rows, :] = with_shift(jnp.zeros((ROW_BLOCK, LANES), jnp.float32), shift)

    each_row_block(q_ref, begin)
    step_kernel(q_ref, kv_ref, acc_ref, acc_ref)


def each_row_block(q_ref, step, size=ROW_BLOCK):
    def body(i, carry):
        step(pl.ds(pl.multiple_of(i * size, size), size))
        return carry

    lax.fori_loop(0, q_ref.shape[0] // size, body, 0)


def step_kernel(q_ref, kv_ref, acc_in_ref, acc_ref):
    keys, values = keys_twice(kv_ref[...]), values_and_one(kv_ref[...])

    def one(rows):
        acc = acc_in_ref[rows, :]
        p = jnp.exp2(scores(q_ref, rows, keys) - acc[:, SHIFT:]).astype(jnp.bfloat16)
        acc_ref[rows, :] = acc + jnp.dot(p, values, preferred_element_type=jnp.float32)

    each_row_block(q_ref, one)


def last_kernel(q_ref, kv_ref, acc_in_ref, *refs):
    kv_refs, (acc_ref, kv_buf, sem) = refs[:-3], refs[-3:]
    step_kernel(q_ref, kv_ref, acc_in_ref, acc_ref)
    outside = jnp.where(acc_ref[...] < BIG, 0.0, 1.0)
    fine = jnp.max(jnp.sum(outside, axis=0, keepdims=True)) < 0.5

    @pl.when(jnp.logical_not(fine))
    def _():
        acc_ref[...] = with_shift(jnp.zeros_like(acc_ref), LOWEST)
        for other_kv_ref in kv_refs:
            copy = pltpu.make_async_copy(other_kv_ref, kv_buf, sem)
            copy.start()
            copy.wait()
            redo_block(q_ref, kv_buf, acc_ref)


def redo_block(q_ref, kv_ref, acc_ref):
    keys, values = keys_twice(kv_ref[...]), values_and_one(kv_ref[...])

    def one(rows):
        s = scores(q_ref, rows, keys)
        acc = acc_ref[rows, :]
        before = acc[:, SHIFT:]
        highest = jnp.maximum(jnp.max(s, axis=1, keepdims=True), before)
        p = jnp.exp2(s - highest).astype(jnp.bfloat16)
        contrib = jnp.dot(p, values, preferred_element_type=jnp.float32)
        acc_ref[rows, :] = with_shift(acc * jnp.exp2(before - highest) + contrib, highest)

    each_row_block(q_ref, one, REDO_BLOCK)


def merge_kernel(own_ref, other_ref, out_ref):
    own, other = own_ref[...], other_ref[...]
    a, b = own[:, SHIFT:], other[:, SHIFT:]
    top = jnp.maximum(a, b)
    both = own * jnp.exp2(a - top) + other * jnp.exp2(b - top)
    attended = (both[:, :HEAD_DIM] / both[:, STAT : STAT + 1]).astype(jnp.bfloat16)
    half = attended.shape[0] // 2
    out_ref[...] = jnp.concatenate([attended[:half], attended[half:]], axis=1).reshape(
        out_ref.shape
    )


def project_kernel(heads_ref, w_ref, out_ref):
    left = [heads_ref[h][:, :HEAD_DIM] for h in range(HEADS)]
    right = [heads_ref[h][:, HEAD_DIM:] for h in range(HEADS)]
    attended = jnp.concatenate(
        [jnp.concatenate(left, axis=1), jnp.concatenate(right, axis=1)], axis=0
    )
    out_ref[...] = jnp.dot(attended, w_ref[...], preferred_element_type=jnp.float32).astype(
        jnp.bfloat16
    )


def call(kernel, *shapes, vmem=24, **more):
    return pl.pallas_call(
        kernel,
        out_shape=shapes if len(shapes) > 1 else shapes[0],
        compiler_params=pltpu.CompilerParams(vmem_limit_bytes=vmem * 2**20),
        **more,
    )


def on_device(q, k, v, w_out):
    rows, width = q.shape
    half = rows // 2
    bf16, f32 = jnp.bfloat16, jnp.float32
    shape = jax.ShapeDtypeStruct
    vmem = pl.BlockSpec(memory_space=pltpu.VMEM)
    anywhere = pl.BlockSpec(memory_space=pl.ANY)

    packed = call(
        pack_kernel,
        shape((HEADS, rows + half, LANES), bf16),
        vmem=56,
        in_specs=[anywhere] * 3,
        out_specs=vmem,
        scratch_shapes=[pltpu.VMEM((rows, width), bf16)] * 3 + [pltpu.SemaphoreType.DMA((3,))],
    )(q, k, v)
    mine = lax.all_to_all(packed, ("x", "y"), 0, 0, tiled=True)
    swap = [(0, 1), (1, 0)]
    count = HEADS * rows
    kv = mine[:, :rows].reshape(count, LANES)

    deep = lax.axis_size("zh") * lax.axis_size("zl")
    pairings = (
        lambda z: z ^ 1,
        lambda z: (z + 1) % deep if z % 2 else (z - 1) % deep,
    )

    def exchanged(block, hop):
        pairs = [
            (2 * z + c, 2 * pairings[(hop + c) % 2](z) + c) for z in range(deep) for c in range(2)
        ]
        return lax.ppermute(block, ("zh", "zl", "c"), pairs)

    def cost(blocks):
        return pl.CostEstimate(
            flops=2 * 2 * 2 * count * count * 2 * LANES * blocks,
            bytes_accessed=4 * 2**20,
            transcendentals=2 * count * count * blocks,
        )

    q_shape, acc_shape = shape((2 * count, LANES), bf16), shape((2 * count, LANES), f32)
    chains = [exchanged(kv, 0)]
    partners = lax.ppermute(mine, "c", swap)
    chains.append(exchanged(partners[:, :rows].reshape(count, LANES), 0))
    q_all, acc = call(first_kernel, q_shape, acc_shape, cost_estimate=cost(1))(
        mine[:, rows:], partners[:, rows:], kv
    )
    blocks = [kv]
    for hop in range(1, deep // 2):
        for n in range(2):
            now, acc = lax.optimization_barrier((chains[n], acc))
            blocks.append(now)
            if n == 0 or hop + 1 < deep // 2:
                chains[n] = exchanged(now, hop)
            acc = call(
                step_kernel, acc_shape, cost_estimate=cost(1), input_output_aliases={2: 0}
            )(q_all, now, acc)
    blocks.append(chains[0])
    acc = call(
        last_kernel,
        acc_shape,
        in_specs=[vmem] * 3 + [anywhere] * len(blocks),
        out_specs=vmem,
        scratch_shapes=[pltpu.VMEM((count, LANES), bf16), pltpu.SemaphoreType.DMA],
        cost_estimate=cost(1),
        input_output_aliases={2: 0},
    )(q_all, chains[0], acc, *blocks)
    arrived = lax.ppermute(acc[count:], "c", swap)
    own = acc[:count]
    attended = call(merge_kernel, shape((HEADS, half, LANES), bf16))(own, arrived)
    heads = lax.all_to_all(attended, ("x", "y"), 0, 0, tiled=True)
    return call(project_kernel, shape((rows, width), bf16))(heads, w_out)


def solution(mesh):
    axes = ("x", "y", "zh", "zl", "c")
    fine = Mesh(mesh.devices.reshape(4, 4, 2, 4, 2), axes)
    return jax.shard_map(
        on_device,
        mesh=fine,
        in_specs=(P(axes, None), P(axes, None), P(axes, None), P()),
        out_specs=P(axes, None),
        check_vma=False,
    )
```

```python
import functools

import jax
import jax.numpy as jnp
from jax import lax
from jax.experimental import pallas as pl
from jax.experimental.pallas import tpu as pltpu
from jax.sharding import Mesh, PartitionSpec as P

HEADS = 16
HEAD_DIM = 64
LANES = 128
STAT = HEAD_DIM
SHIFT = LANES - 1
LOG2E = 1.4426950408889634
BIG = 2.0**100
LOWEST = -1e30
ROW_BLOCK = 1024
REDO_BLOCK = 256
SHIFT_KEYS = 128

NT = (((1,), (1,)), ((), ()))


def pack_kernel(q_hbm, k_hbm, v_hbm, out_ref, q_ref, k_ref, v_ref, sem):
    rows = q_ref.shape[0]
    half = rows // 2
    copies = [
        pltpu.make_async_copy(source, target, sem.at[n])
        for n, (source, target) in enumerate(((k_hbm, k_ref), (v_hbm, v_ref), (q_hbm, q_ref)))
    ]
    for copy in copies:
        copy.start()
    for copy in copies:
        copy.wait()
    for head in range(HEADS):
        cols = slice(head * HEAD_DIM, (head + 1) * HEAD_DIM)
        out_ref[head, :rows, :] = jnp.concatenate([k_ref[:, cols], v_ref[:, cols]], axis=1)
        q = q_ref[:, cols]
        out_ref[head, rows:, :] = jnp.concatenate([q[:half], q[half:]], axis=1)


def split_queries(q):
    stacked = jnp.concatenate([q[:, :HEAD_DIM], q[:, HEAD_DIM:]], axis=0).astype(jnp.float32)
    scaled = stacked * (LOG2E * HEAD_DIM**-0.5)
    high = scaled.astype(jnp.bfloat16)
    low = (scaled - high.astype(jnp.float32)).astype(jnp.bfloat16)
    return jnp.concatenate([high, low], axis=1)


def keys_twice(kv):
    return jnp.concatenate([kv[:, :HEAD_DIM], kv[:, :HEAD_DIM]], axis=1)


def values_and_one(kv):
    lane = lax.broadcasted_iota(jnp.int32, (kv.shape[0], HEAD_DIM), 1)
    one = jnp.where(lane == 0, 1.0, 0.0).astype(kv.dtype)
    return jnp.concatenate([kv[:, HEAD_DIM:], one], axis=1)


def with_shift(acc, shift):
    lane = lax.broadcasted_iota(jnp.int32, acc.shape, 1)
    return jnp.where(lane == SHIFT, shift, acc)


def scores(q_ref, rows, keys):
    return lax.dot_general(q_ref[rows, :], keys, NT, preferred_element_type=jnp.float32)


def first_kernel(q_own_ref, q_other_ref, kv_ref, q_ref, acc_ref):
    heads, rows, _ = q_own_ref.shape
    count = 2 * heads * rows
    q_ref[:count, :] = split_queries(q_own_ref[...].reshape(heads * rows, LANES))
    q_ref[count:, :] = split_queries(q_other_ref[...].reshape(heads * rows, LANES))
    few = keys_twice(kv_ref[:SHIFT_KEYS, :])

    def begin(rows):
        shift = jnp.max(scores(q_ref, rows, few), axis=1, keepdims=True)
        acc_ref[rows, :] = with_shift(jnp.zeros((ROW_BLOCK, LANES), jnp.float32), shift)

    each_row_block(q_ref, begin)
    step_kernel(q_ref, kv_ref, acc_ref, acc_ref)


def each_row_block(q_ref, step, size=ROW_BLOCK):
    def body(i, carry):
        step(pl.ds(pl.multiple_of(i * size, size), size))
        return carry

    lax.fori_loop(0, q_ref.shape[0] // size, body, 0)


def step_kernel(q_ref, kv_ref, acc_in_ref, acc_ref):
    keys, values = keys_twice(kv_ref[...]), values_and_one(kv_ref[...])

    def one(rows):
        acc = acc_in_ref[rows, :]
        p = jnp.exp2(scores(q_ref, rows, keys) - acc[:, SHIFT:]).astype(jnp.bfloat16)
        acc_ref[rows, :] = acc + jnp.dot(p, values, preferred_element_type=jnp.float32)

    each_row_block(q_ref, one)


def last_kernel(q_ref, kv_ref, acc_in_ref, *refs):
    kv_refs, (acc_ref, kv_buf, sem) = refs[:-3], refs[-3:]
    step_kernel(q_ref, kv_ref, acc_in_ref, acc_ref)
    outside = jnp.where(acc_ref[...] < BIG, 0.0, 1.0)
    fine = jnp.max(jnp.sum(outside, axis=0, keepdims=True)) < 0.5

    @pl.when(jnp.logical_not(fine))
    def _():
        acc_ref[...] = with_shift(jnp.zeros_like(acc_ref), LOWEST)
        for n, other_kv_ref in enumerate(kv_refs):
            copy = pltpu.make_async_copy(other_kv_ref, kv_buf.at[n], sem)
            copy.start()
            copy.wait()

        def redo(n, carry):
            redo_block(q_ref, kv_buf.at[n], acc_ref)
            return carry

        lax.fori_loop(0, len(kv_refs), redo, 0)


def redo_block(q_ref, kv_ref, acc_ref):
    keys, values = keys_twice(kv_ref[...]), values_and_one(kv_ref[...])

    def one(rows):
        s = scores(q_ref, rows, keys)
        acc = acc_ref[rows, :]
        before = acc[:, SHIFT:]
        highest = jnp.maximum(jnp.max(s, axis=1, keepdims=True), before)
        p = jnp.exp2(s - highest).astype(jnp.bfloat16)
        contrib = jnp.dot(p, values, preferred_element_type=jnp.float32)
        acc_ref[rows, :] = with_shift(acc * jnp.exp2(before - highest) + contrib, highest)

    each_row_block(q_ref, one, REDO_BLOCK)


def merge_kernel(own_ref, other_ref, out_ref):
    own, other = own_ref[...], other_ref[...]
    a, b = own[:, SHIFT:], other[:, SHIFT:]
    top = jnp.maximum(a, b)
    both = own * jnp.exp2(a - top) + other * jnp.exp2(b - top)
    attended = (both[:, :HEAD_DIM] / both[:, STAT : STAT + 1]).astype(jnp.bfloat16)
    half = attended.shape[0] // 2
    out_ref[...] = jnp.concatenate([attended[:half], attended[half:]], axis=1).reshape(
        out_ref.shape
    )


def project_kernel(heads_ref, w_ref, out_ref):
    left = [heads_ref[h][:, :HEAD_DIM] for h in range(HEADS)]
    right = [heads_ref[h][:, HEAD_DIM:] for h in range(HEADS)]
    attended = jnp.concatenate(
        [jnp.concatenate(left, axis=1), jnp.concatenate(right, axis=1)], axis=0
    )
    out_ref[...] = jnp.dot(attended, w_ref[...], preferred_element_type=jnp.float32).astype(
        jnp.bfloat16
    )


def call(kernel, *shapes, vmem=24, **more):
    return pl.pallas_call(
        kernel,
        out_shape=shapes if len(shapes) > 1 else shapes[0],
        compiler_params=pltpu.CompilerParams(vmem_limit_bytes=vmem * 2**20),
        **more,
    )


def on_device(q, k, v, w_out):
    rows, width = q.shape
    half = rows // 2
    bf16, f32 = jnp.bfloat16, jnp.float32
    shape = jax.ShapeDtypeStruct
    vmem = pl.BlockSpec(memory_space=pltpu.VMEM)
    anywhere = pl.BlockSpec(memory_space=pl.ANY)

    packed = call(
        pack_kernel,
        shape((HEADS, rows + half, LANES), bf16),
        vmem=56,
        in_specs=[anywhere] * 3,
        out_specs=vmem,
        scratch_shapes=[pltpu.VMEM((rows, width), bf16)] * 3 + [pltpu.SemaphoreType.DMA((3,))],
    )(q, k, v)
    mine = lax.all_to_all(packed, ("x", "y"), 0, 0, tiled=True)
    swap = [(0, 1), (1, 0)]
    count = HEADS * rows
    kv = mine[:, :rows].reshape(count, LANES)

    deep = lax.axis_size("zh") * lax.axis_size("zl")
    pairings = (
        lambda z: z ^ 1,
        lambda z: (z + 1) % deep if z % 2 else (z - 1) % deep,
    )

    def exchanged(block, hop):
        pairs = [
            (2 * z + c, 2 * pairings[(hop + c) % 2](z) + c) for z in range(deep) for c in range(2)
        ]
        return lax.ppermute(block, ("zh", "zl", "c"), pairs)

    def cost(blocks):
        return pl.CostEstimate(
            flops=2 * 2 * 2 * count * count * 2 * LANES * blocks,
            bytes_accessed=4 * 2**20,
            transcendentals=2 * count * count * blocks,
        )

    q_shape, acc_shape = shape((2 * count, LANES), bf16), shape((2 * count, LANES), f32)
    chains = [exchanged(kv, 0)]
    partners = lax.ppermute(mine, "c", swap)
    chains.append(exchanged(partners[:, :rows].reshape(count, LANES), 0))
    q_all, acc = call(first_kernel, q_shape, acc_shape, cost_estimate=cost(1))(
        mine[:, rows:], partners[:, rows:], kv
    )
    blocks = [kv]
    for hop in range(1, deep // 2):
        for n in range(2):
            now, acc = lax.optimization_barrier((chains[n], acc))
            blocks.append(now)
            if n == 0 or hop + 1 < deep // 2:
                chains[n] = exchanged(now, hop)
            acc = call(
                step_kernel, acc_shape, cost_estimate=cost(1), input_output_aliases={2: 0}
            )(q_all, now, acc)
    blocks.append(chains[0])
    acc = call(
        last_kernel,
        acc_shape,
        in_specs=[vmem] * 3 + [anywhere] * len(blocks),
        out_specs=vmem,
        scratch_shapes=[pltpu.VMEM((len(blocks), count, LANES), bf16), pltpu.SemaphoreType.DMA],
        cost_estimate=cost(1),
        input_output_aliases={2: 0},
    )(q_all, chains[0], acc, *blocks)
    arrived = lax.ppermute(acc[count:], "c", swap)
    own = acc[:count]
    attended = call(merge_kernel, shape((HEADS, half, LANES), bf16))(own, arrived)
    heads = lax.all_to_all(attended, ("x", "y"), 0, 0, tiled=True)
    return call(project_kernel, shape((rows, width), bf16))(heads, w_out)


def solution(mesh):
    axes = ("x", "y", "zh", "zl", "c")
    fine = Mesh(mesh.devices.reshape(4, 4, 2, 4, 2), axes)
    return jax.shard_map(
        on_device,
        mesh=fine,
        in_specs=(P(axes, None), P(axes, None), P(axes, None), P()),
        out_specs=P(axes, None),
        check_vma=False,
    )
```

```python
import functools

import jax
import jax.numpy as jnp
from jax import lax
from jax.experimental import pallas as pl
from jax.experimental.pallas import tpu as pltpu
from jax.sharding import Mesh, PartitionSpec as P

HEADS = 16
HEAD_DIM = 64
LANES = 128
STAT = HEAD_DIM
SHIFT = LANES - 1
LOG2E = 1.4426950408889634
BIG = 2.0**100
LOWEST = -1e30
ROW_BLOCK = 1024
REDO_BLOCK = 256
SHIFT_KEYS = 128

NT = (((1,), (1,)), ((), ()))


def pack_kernel(q_hbm, k_hbm, v_hbm, out_ref, q_ref, k_ref, v_ref, sem):
    rows = q_ref.shape[0]
    half = rows // 2
    copies = [
        pltpu.make_async_copy(source, target, sem.at[n])
        for n, (source, target) in enumerate(((k_hbm, k_ref), (v_hbm, v_ref), (q_hbm, q_ref)))
    ]
    for copy in copies:
        copy.start()
    for copy in copies:
        copy.wait()
    for head in range(HEADS):
        cols = slice(head * HEAD_DIM, (head + 1) * HEAD_DIM)
        out_ref[head, :rows, :] = jnp.concatenate([k_ref[:, cols], v_ref[:, cols]], axis=1)
        q = q_ref[:, cols]
        out_ref[head, rows:, :] = jnp.concatenate([q[:half], q[half:]], axis=1)


def split_queries(q):
    stacked = jnp.concatenate([q[:, :HEAD_DIM], q[:, HEAD_DIM:]], axis=0).astype(jnp.float32)
    scaled = stacked * (LOG2E * HEAD_DIM**-0.5)
    high = scaled.astype(jnp.bfloat16)
    low = (scaled - high.astype(jnp.float32)).astype(jnp.bfloat16)
    return jnp.concatenate([high, low], axis=1)


def keys_twice(kv):
    return jnp.concatenate([kv[:, :HEAD_DIM], kv[:, :HEAD_DIM]], axis=1)


def values_and_one(kv):
    lane = lax.broadcasted_iota(jnp.int32, (kv.shape[0], HEAD_DIM), 1)
    one = jnp.where(lane == 0, 1.0, 0.0).astype(kv.dtype)
    return jnp.concatenate([kv[:, HEAD_DIM:], one], axis=1)


def with_shift(acc, shift):
    lane = lax.broadcasted_iota(jnp.int32, acc.shape, 1)
    return jnp.where(lane == SHIFT, shift, acc)


def scores(q_ref, rows, keys):
    return lax.dot_general(q_ref[rows, :], keys, NT, preferred_element_type=jnp.float32)


def first_kernel(q_own_ref, q_other_ref, kv_ref, q_ref, acc_ref):
    heads, rows, _ = q_own_ref.shape
    count = 2 * heads * rows
    q_ref[:count, :] = split_queries(q_own_ref[...].reshape(heads * rows, LANES))
    q_ref[count:, :] = split_queries(q_other_ref[...].reshape(heads * rows, LANES))
    few = keys_twice(kv_ref[:SHIFT_KEYS, :])

    def begin(rows):
        shift = jnp.max(scores(q_ref, rows, few), axis=1, keepdims=True)
        acc_ref[rows, :] = with_shift(jnp.zeros((ROW_BLOCK, LANES), jnp.float32), shift)

    each_row_block(q_ref, begin)
    step_kernel(q_ref, kv_ref, acc_ref, acc_ref)


def each_row_block(q_ref, step, size=ROW_BLOCK):
    def body(i, carry):
        step(pl.ds(pl.multiple_of(i * size, size), size))
        return carry

    lax.fori_loop(0, q_ref.shape[0] // size, body, 0)


def step_kernel(q_ref, kv_ref, acc_in_ref, acc_ref):
    keys, values = keys_twice(kv_ref[...]), values_and_one(kv_ref[...])

    def one(rows):
        acc = acc_in_ref[rows, :]
        p = jnp.exp2(scores(q_ref, rows, keys) - acc[:, SHIFT:]).astype(jnp.bfloat16)
        acc_ref[rows, :] = acc + jnp.dot(p, values, preferred_element_type=jnp.float32)

    each_row_block(q_ref, one)


def last_kernel(q_ref, kv_ref, acc_in_ref, *refs):
    kv_refs, (acc_ref, kv_buf, sem) = refs[:-3], refs[-3:]
    step_kernel(q_ref, kv_ref, acc_in_ref, acc_ref)
    outside = jnp.where(acc_ref[...] < BIG, 0.0, 1.0)
    fine = jnp.max(jnp.sum(outside, axis=0, keepdims=True)) < 0.5

    @pl.when(jnp.logical_not(fine))
    def _():
        acc_ref[...] = with_shift(jnp.zeros_like(acc_ref), LOWEST)
        for other_kv_ref in kv_refs:
            copy = pltpu.make_async_copy(other_kv_ref, kv_buf, sem)
            copy.start()
            copy.wait()
            redo_block(q_ref, kv_buf, acc_ref)


def redo_block(q_ref, kv_ref, acc_ref):
    keys, values = keys_twice(kv_ref[...]), values_and_one(kv_ref[...])

    def one(rows):
        s = scores(q_ref, rows, keys)
        acc = acc_ref[rows, :]
        before = acc[:, SHIFT:]
        highest = jnp.maximum(jnp.max(s, axis=1, keepdims=True), before)
        p = jnp.exp2(s - highest).astype(jnp.bfloat16)
        contrib = jnp.dot(p, values, preferred_element_type=jnp.float32)
        acc_ref[rows, :] = with_shift(acc * jnp.exp2(before - highest) + contrib, highest)

    each_row_block(q_ref, one, REDO_BLOCK)


def merge_kernel(own_ref, other_ref, out_ref):
    own, other = own_ref[...], other_ref[...]
    a, b = own[:, SHIFT:], other[:, SHIFT:]
    top = jnp.maximum(a, b)
    both = own * jnp.exp2(a - top) + other * jnp.exp2(b - top)
    attended = (both[:, :HEAD_DIM] / both[:, STAT : STAT + 1]).astype(jnp.bfloat16)
    half = attended.shape[0] // 2
    out_ref[...] = jnp.concatenate([attended[:half], attended[half:]], axis=1).reshape(
        out_ref.shape
    )


def project_kernel(heads_ref, w_ref, out_ref):
    left = [heads_ref[h][:, :HEAD_DIM] for h in range(HEADS)]
    right = [heads_ref[h][:, HEAD_DIM:] for h in range(HEADS)]
    attended = jnp.concatenate(
        [jnp.concatenate(left, axis=1), jnp.concatenate(right, axis=1)], axis=0
    )
    out_ref[...] = jnp.dot(attended, w_ref[...], preferred_element_type=jnp.float32).astype(
        jnp.bfloat16
    )


def call(kernel, *shapes, vmem=24, **more):
    return pl.pallas_call(
        kernel,
        out_shape=shapes if len(shapes) > 1 else shapes[0],
        compiler_params=pltpu.CompilerParams(vmem_limit_bytes=vmem * 2**20),
        **more,
    )


def on_device(q, k, v, w_out):
    rows, width = q.shape
    half = rows // 2
    bf16, f32 = jnp.bfloat16, jnp.float32
    shape = jax.ShapeDtypeStruct
    vmem = pl.BlockSpec(memory_space=pltpu.VMEM)
    anywhere = pl.BlockSpec(memory_space=pl.ANY)

    packed = call(
        pack_kernel,
        shape((HEADS, rows + half, LANES), bf16),
        vmem=56,
        in_specs=[anywhere] * 3,
        out_specs=vmem,
        scratch_shapes=[pltpu.VMEM((rows, width), bf16)] * 3 + [pltpu.SemaphoreType.DMA((3,))],
    )(q, k, v)
    mine = lax.all_to_all(packed, ("x", "y"), 0, 0, tiled=True)
    swap = [(0, 1), (1, 0)]
    count = HEADS * rows
    kv = mine[:, :rows].reshape(count, LANES)

    deep = lax.axis_size("zh") * lax.axis_size("zl")
    pairings = (
        lambda z: z ^ 1,
        lambda z: (z + 1) % deep if z % 2 else (z - 1) % deep,
    )

    def exchanged(block, turn):
        pairs = [(z, pairings[turn % 2](z)) for z in range(deep)]
        return lax.ppermute(block, ("zh", "zl"), pairs)

    def cost(blocks):
        return pl.CostEstimate(
            flops=2 * 2 * 2 * count * count * 2 * LANES * blocks,
            bytes_accessed=4 * 2**20,
            transcendentals=2 * count * count * blocks,
        )

    q_shape, acc_shape = shape((2 * count, LANES), bf16), shape((2 * count, LANES), f32)
    chains = [exchanged(kv, 0)]
    partners = lax.ppermute(mine, "c", swap)
    chains.append(exchanged(partners[:, :rows].reshape(count, LANES), 1))
    q_all, acc = call(first_kernel, q_shape, acc_shape, cost_estimate=cost(1))(
        mine[:, rows:], partners[:, rows:], kv
    )
    blocks = [kv]
    for hop in range(1, deep // 2):
        for n in range(2):
            now, acc = lax.optimization_barrier((chains[n], acc))
            blocks.append(now)
            if n == 0 or hop + 1 < deep // 2:
                chains[n] = exchanged(now, hop + n)
            acc = call(
                step_kernel, acc_shape, cost_estimate=cost(1), input_output_aliases={2: 0}
            )(q_all, now, acc)
    blocks.append(chains[0])
    acc = call(
        last_kernel,
        acc_shape,
        in_specs=[vmem] * 3 + [anywhere] * len(blocks),
        out_specs=vmem,
        scratch_shapes=[pltpu.VMEM((count, LANES), bf16), pltpu.SemaphoreType.DMA],
        cost_estimate=cost(1),
        input_output_aliases={2: 0},
    )(q_all, chains[0], acc, *blocks)
    arrived = lax.ppermute(acc[count:], "c", swap)
    own = acc[:count]
    attended = call(merge_kernel, shape((HEADS, half, LANES), bf16))(own, arrived)
    heads = lax.all_to_all(attended, ("x", "y"), 0, 0, tiled=True)
    return call(project_kernel, shape((rows, width), bf16))(heads, w_out)


def solution(mesh):
    axes = ("x", "y", "zh", "zl", "c")
    fine = Mesh(mesh.devices.reshape(4, 4, 2, 4, 2), axes)
    return jax.shard_map(
        on_device,
        mesh=fine,
        in_specs=(P(axes, None), P(axes, None), P(axes, None), P()),
        out_specs=P(axes, None),
        check_vma=False,
    )
```

```python
import functools

import jax
import jax.numpy as jnp
from jax import lax
from jax.experimental import pallas as pl
from jax.experimental.pallas import tpu as pltpu
from jax.sharding import Mesh, PartitionSpec as P

HEADS = 16
HEAD_DIM = 64
LANES = 128
STAT = HEAD_DIM
SHIFT = LANES - 1
LOG2E = 1.4426950408889634
BIG = 2.0**100
LOWEST = -1e30
ROW_BLOCK = 1024
REDO_BLOCK = 256
SHIFT_KEYS = 128

NT = (((1,), (1,)), ((), ()))


def pack_kernel(q_hbm, k_hbm, v_hbm, out_ref, q_ref, k_ref, v_ref, sem):
    rows = q_ref.shape[0]
    half = rows // 2
    copies = [
        pltpu.make_async_copy(source, target, sem.at[n])
        for n, (source, target) in enumerate(((k_hbm, k_ref), (v_hbm, v_ref), (q_hbm, q_ref)))
    ]
    for copy in copies:
        copy.start()
    for copy in copies:
        copy.wait()
    for head in range(HEADS):
        cols = slice(head * HEAD_DIM, (head + 1) * HEAD_DIM)
        out_ref[head, :rows, :] = jnp.concatenate([k_ref[:, cols], v_ref[:, cols]], axis=1)
        q = q_ref[:, cols]
        out_ref[head, rows:, :] = jnp.concatenate([q[:half], q[half:]], axis=1)


def split_queries(q):
    stacked = jnp.concatenate([q[:, :HEAD_DIM], q[:, HEAD_DIM:]], axis=0).astype(jnp.float32)
    scaled = stacked * (LOG2E * HEAD_DIM**-0.5)
    high = scaled.astype(jnp.bfloat16)
    low = (scaled - high.astype(jnp.float32)).astype(jnp.bfloat16)
    return jnp.concatenate([high, low], axis=1)


def keys_twice(kv):
    return jnp.concatenate([kv[:, :HEAD_DIM], kv[:, :HEAD_DIM]], axis=1)


def values_and_one(kv):
    lane = lax.broadcasted_iota(jnp.int32, (kv.shape[0], HEAD_DIM), 1)
    one = jnp.where(lane == 0, 1.0, 0.0).astype(kv.dtype)
    return jnp.concatenate([kv[:, HEAD_DIM:], one], axis=1)


def with_shift(acc, shift):
    lane = lax.broadcasted_iota(jnp.int32, acc.shape, 1)
    return jnp.where(lane == SHIFT, shift, acc)


def scores(q_ref, rows, keys):
    return lax.dot_general(q_ref[rows, :], keys, NT, preferred_element_type=jnp.float32)


def first_kernel(q_own_ref, q_other_ref, kv_ref, q_ref, acc_ref):
    heads, rows, _ = q_own_ref.shape
    count = 2 * heads * rows
    q_ref[:count, :] = split_queries(q_own_ref[...].reshape(heads * rows, LANES))
    q_ref[count:, :] = split_queries(q_other_ref[...].reshape(heads * rows, LANES))
    few = keys_twice(kv_ref[:SHIFT_KEYS, :])

    def begin(rows):
        shift = jnp.max(scores(q_ref, rows, few), axis=1, keepdims=True)
        acc_ref[rows, :] = with_shift(jnp.zeros((ROW_BLOCK, LANES), jnp.float32), shift)

    each_row_block(q_ref, begin)
    step_kernel(q_ref, kv_ref, acc_ref, acc_ref)


def each_row_block(q_ref, step, size=ROW_BLOCK):
    def body(i, carry):
        step(pl.ds(pl.multiple_of(i * size, size), size))
        return carry

    lax.fori_loop(0, q_ref.shape[0] // size, body, 0)


def step_kernel(q_ref, kv_ref, acc_in_ref, acc_ref):
    keys, values = keys_twice(kv_ref[...]), values_and_one(kv_ref[...])

    def one(rows):
        acc = acc_in_ref[rows, :]
        p = jnp.exp2(scores(q_ref, rows, keys) - acc[:, SHIFT:]).astype(jnp.bfloat16)
        acc_ref[rows, :] = acc + jnp.dot(p, values, preferred_element_type=jnp.float32)

    each_row_block(q_ref, one)


def last_kernel(q_ref, kv_ref, acc_in_ref, *refs):
    kv_refs, (acc_ref, kv_buf, sem) = refs[:-3], refs[-3:]
    step_kernel(q_ref, kv_ref, acc_in_ref, acc_ref)
    outside = jnp.where(acc_ref[...] < BIG, 0.0, 1.0)
    fine = jnp.max(jnp.sum(outside, axis=0, keepdims=True)) < 0.5

    @pl.when(jnp.logical_not(fine))
    def _():
        acc_ref[...] = with_shift(jnp.zeros_like(acc_ref), LOWEST)
        for n, other_kv_ref in enumerate(kv_refs):
            copy = pltpu.make_async_copy(other_kv_ref, kv_buf.at[n], sem)
            copy.start()
            copy.wait()

        def redo(n, carry):
            redo_block(q_ref, kv_buf.at[n], acc_ref)
            return carry

        lax.fori_loop(0, len(kv_refs), redo, 0)


def redo_block(q_ref, kv_ref, acc_ref):
    keys, values = keys_twice(kv_ref[...]), values_and_one(kv_ref[...])

    def one(rows):
        s = scores(q_ref, rows, keys)
        acc = acc_ref[rows, :]
        before = acc[:, SHIFT:]
        highest = jnp.maximum(jnp.max(s, axis=1, keepdims=True), before)
        p = jnp.exp2(s - highest).astype(jnp.bfloat16)
        contrib = jnp.dot(p, values, preferred_element_type=jnp.float32)
        acc_ref[rows, :] = with_shift(acc * jnp.exp2(before - highest) + contrib, highest)

    each_row_block(q_ref, one, REDO_BLOCK)


def merge_kernel(own_ref, other_ref, out_ref):
    own, other = own_ref[...], other_ref[...]
    a, b = own[:, SHIFT:], other[:, SHIFT:]
    top = jnp.maximum(a, b)
    both = own * jnp.exp2(a - top) + other * jnp.exp2(b - top)
    attended = (both[:, :HEAD_DIM] / both[:, STAT : STAT + 1]).astype(jnp.bfloat16)
    half = attended.shape[0] // 2
    out_ref[...] = jnp.concatenate([attended[:half], attended[half:]], axis=1).reshape(
        out_ref.shape
    )


def project_kernel(heads_ref, w_ref, out_ref):
    left = [heads_ref[h][:, :HEAD_DIM] for h in range(HEADS)]
    right = [heads_ref[h][:, HEAD_DIM:] for h in range(HEADS)]
    attended = jnp.concatenate(
        [jnp.concatenate(left, axis=1), jnp.concatenate(right, axis=1)], axis=0
    )
    out_ref[...] = jnp.dot(attended, w_ref[...], preferred_element_type=jnp.float32).astype(
        jnp.bfloat16
    )


def call(kernel, *shapes, vmem=24, **more):
    return pl.pallas_call(
        kernel,
        out_shape=shapes if len(shapes) > 1 else shapes[0],
        compiler_params=pltpu.CompilerParams(vmem_limit_bytes=vmem * 2**20),
        **more,
    )


def on_device(q, k, v, w_out):
    rows, width = q.shape
    half = rows // 2
    bf16, f32 = jnp.bfloat16, jnp.float32
    shape = jax.ShapeDtypeStruct
    vmem = pl.BlockSpec(memory_space=pltpu.VMEM)
    anywhere = pl.BlockSpec(memory_space=pl.ANY)

    packed = call(
        pack_kernel,
        shape((HEADS, rows + half, LANES), bf16),
        vmem=56,
        in_specs=[anywhere] * 3,
        out_specs=vmem,
        scratch_shapes=[pltpu.VMEM((rows, width), bf16)] * 3 + [pltpu.SemaphoreType.DMA((3,))],
    )(q, k, v)
    mine = lax.all_to_all(packed, ("x", "y"), 0, 0, tiled=True)
    swap = [(0, 1), (1, 0)]
    count = HEADS * rows
    kv = mine[:, :rows].reshape(count, LANES)

    deep = lax.axis_size("zh") * lax.axis_size("zl")
    pairings = (
        lambda z: z ^ 1,
        lambda z: (z + 1) % deep if z % 2 else (z - 1) % deep,
    )

    def exchanged(block, hop):
        pairs = [
            (2 * z + c, 2 * pairings[(hop + c) % 2](z) + c) for z in range(deep) for c in range(2)
        ]
        return lax.ppermute(block, ("zh", "zl", "c"), pairs)

    def cost(blocks):
        return pl.CostEstimate(
            flops=2 * 2 * 2 * count * count * 2 * LANES * blocks,
            bytes_accessed=4 * 2**20,
            transcendentals=2 * count * count * blocks,
        )

    q_shape, acc_shape = shape((2 * count, LANES), bf16), shape((2 * count, LANES), f32)
    chains = [exchanged(kv, 0)]
    partner_kv = lax.ppermute(kv, "c", swap)
    partner_q = lax.ppermute(mine[:, rows:], "c", swap)
    chains.append(exchanged(partner_kv, 0))
    q_all, acc = call(first_kernel, q_shape, acc_shape, cost_estimate=cost(1))(
        mine[:, rows:], partner_q, kv
    )
    blocks = [kv]
    for hop in range(1, deep // 2):
        for n in range(2):
            now, acc = lax.optimization_barrier((chains[n], acc))
            blocks.append(now)
            if n == 0 or hop + 1 < deep // 2:
                chains[n] = exchanged(now, hop)
            acc = call(
                step_kernel, acc_shape, cost_estimate=cost(1), input_output_aliases={2: 0}
            )(q_all, now, acc)
    blocks.append(chains[0])
    acc = call(
        last_kernel,
        acc_shape,
        in_specs=[vmem] * 3 + [anywhere] * len(blocks),
        out_specs=vmem,
        scratch_shapes=[pltpu.VMEM((len(blocks), count, LANES), bf16), pltpu.SemaphoreType.DMA],
        cost_estimate=cost(1),
        input_output_aliases={2: 0},
    )(q_all, chains[0], acc, *blocks)
    arrived = lax.ppermute(acc[count:], "c", swap)
    own = acc[:count]
    attended = call(merge_kernel, shape((HEADS, half, LANES), bf16))(own, arrived)
    heads = lax.all_to_all(attended, ("x", "y"), 0, 0, tiled=True)
    return call(project_kernel, shape((rows, width), bf16))(heads, w_out)


def solution(mesh):
    axes = ("x", "y", "zh", "zl", "c")
    fine = Mesh(mesh.devices.reshape(4, 4, 2, 4, 2), axes)
    return jax.shard_map(
        on_device,
        mesh=fine,
        in_specs=(P(axes, None), P(axes, None), P(axes, None), P()),
        out_specs=P(axes, None),
        check_vma=False,
    )
```
